32 devices in a mesh: row: 8 (over y, x, core), col: 4 (over z).
Axes of the slice: x: 2, y: 2, z: 4, core: 2. Of those that a mesh axis runs over, the one named last changes fastest.
Arguments:
- density_matrix: bfloat16 [4096, 4096], P('row', 'col'), may hold values from -1 to 1
- block_mask: int32 [32, 32], P('row', 'col'), may hold values 0 or 1
- cell_group: int32 [256, 256], P('row', 'col'), may hold values from 0 to 31
- electron_shape: float32 [256, 256, 256], P('row', 'col'), may hold values from 0.5 to 20
- ion_charge: float32 [256, 256, 256], P('row', 'col'), may hold values from 0.1 to 6
Outputs:
- next_density: bfloat16 [4096, 4096], P('row', 'col')
- potential: float32 [256, 256, 256], P('row', 'col')
The draws below stay inside these ranges and needn't reach their ends.
All inputs are finite; a program needn't handle non-finite values. No bound on the sum of `block_mask` on one device may be relied on, other than what follows from the above.
Results may differ from the reference program's by a relative error of at most 0.001.
Values may be sent and summed in bfloat16 or wider, within the bound.
A program may use at most 128 MiB of HBM per device.

```python
import jax
import jax.numpy as jnp

GRID = 256
NBLK = 32
ORDER = 4096


def ramp_profile(rise):
    position = jnp.arange(GRID, dtype=jnp.float32) / (GRID - 1)
    return jnp.exp(jnp.log(rise) * position)


def ramp_average(rise):
    factor = rise ** (1.0 / (GRID - 1))
    return (rise ** (GRID / (GRID - 1)) - 1.0) / (GRID * (factor - 1.0))


def rough_field(key):
    return jnp.exp(jax.random.uniform(key, (GRID, GRID, GRID), jnp.float32, jnp.log(0.5), jnp.log(2.0)))


def draw_electron_shape(key, part):
    key = jax.random.fold_in(key, 11)
    rise = 4.0
    ramp = ramp_profile(rise)
    return (ramp[:, None, None] * rough_field(key)).astype(jnp.float32)


def draw_ion_charge(key, part):
    key = jax.random.fold_in(key, 12)
    rise = 4.0
    ramp = ramp_profile(rise) / ramp_average(rise)
    rough_mean = 1.5 / (2.0 * jnp.log(2.0))
    return (ramp[:, None, None] * rough_field(key) / rough_mean).astype(jnp.float32)


def plant(values, own_key, low, top_value):
    spot = [jax.random.randint(jax.random.fold_in(own_key, axis), (), 0, length) for axis, length in enumerate(values.shape)]
    widest = values.shape.index(max(values.shape))
    next_to = spot[:widest] + [(spot[widest] + 1) % values.shape[widest]] + spot[widest + 1:]
    return values.at[tuple(spot)].set(low).at[tuple(next_to)].set(top_value)


def block_levels(rng, shape, shards, low, largest):
    factor_of = 1.0
    for axis_at, blocks in shards:
        heights = jax.random.uniform(jax.random.fold_in(jax.random.fold_in(rng, 6), axis_at), (blocks,), jnp.float32, low / len(shards), largest / len(shards))
        factor_of = factor_of * jnp.repeat(jnp.exp(heights), shape[axis_at] // blocks).reshape((-1,) + (1,) * (len(shape) - 1 - axis_at))
    return factor_of


def centred(key, shape, width, reach, cuts=(), kind=jnp.bfloat16):
    entries = jax.random.normal(key, shape, jnp.float32) * width
    if len(cuts) > 0:
        entries = block_levels(key, shape, cuts, -0.22, 0.18) * entries
    return jnp.clip(entries, min=-reach, max=reach).astype(kind)


def setup_inputs(seed: int = 0) -> dict:
    arg_keys = jax.random.split(jax.random.key(seed), 6)
    return {
        "density_matrix": centred(arg_keys[0], (ORDER, ORDER), (1.41 / ORDER ** 0.25), 1.0, ((0, 8), (1, 4))),
        "block_mask": plant((jax.random.randint(arg_keys[1], (NBLK, NBLK), 0, 4) < 1).astype(jnp.int32), jax.random.fold_in(arg_keys[1], 1), 0, 1),
        "cell_group": plant(jax.random.randint(arg_keys[2], (GRID, GRID), 0, NBLK), jax.random.fold_in(arg_keys[2], 1), 0, NBLK - 1).astype(jnp.int32),
        "electron_shape": draw_electron_shape(jax.random.fold_in(arg_keys[5], 71), 0),
        "ion_charge": draw_ion_charge(jax.random.fold_in(arg_keys[5], 71), 0),
    }


def frequency(count):
    index = jnp.arange(count, dtype=jnp.int32)
    return jnp.where(index > count // 2, index - count, index)


def reference(density_matrix, block_mask, cell_group, electron_shape, ion_charge):
    order = density_matrix.shape[0]
    nblocks = block_mask.shape[0]
    blk = order // nblocks
    keep = block_mask.astype(jnp.bfloat16)[:, None, :, None]
    masked = (density_matrix.reshape(nblocks, blk, nblocks, blk) * keep).reshape(order, order)
    wide = masked.astype(jnp.float32)
    square = jnp.dot(wide, wide, preferred_element_type=jnp.float32)
    keep_wide = block_mask.astype(jnp.float32)[:, None, :, None]
    update = (2.0 * wide - square).reshape(nblocks, blk, nblocks, blk) * keep_wide
    next_density = update.reshape(order, order).astype(jnp.bfloat16)
    population = jnp.sum(jnp.diagonal(square).reshape(nblocks, blk), axis=1)
    weight = population * nblocks / jnp.sum(population)
    grid = electron_shape.shape[0]
    mean_shape = jnp.sum(electron_shape) / (grid * grid * grid)
    cell_weight = weight[cell_group]
    charge = cell_weight[:, :, None] * electron_shape / mean_shape - ion_charge
    spectrum = jnp.fft.fftn(charge)
    freq = frequency(grid)
    scale = 2.0 * jnp.pi / grid
    kvals = (freq.astype(jnp.float32) * scale) ** 2
    ksq = kvals[:, None, None] + kvals[None, :, None] + kvals[None, None, :]
    anchor = (freq[:, None, None] == 0) & (freq[None, :, None] == 0) & (freq[None, None, :] == 0)
    kappa = 8.0 / grid
    kernel = jnp.where(anchor, 0.0, 1.0 / (ksq + kappa * kappa))
    potential = jnp.real(jnp.fft.ifftn(spectrum * kernel)).astype(jnp.float32)
    return next_density, potential
```

```python
import functools

import jax
import jax.numpy as jnp
import ml_dtypes
import numpy as np
from jax import lax
from jax.experimental import pallas as pl
from jax.experimental.pallas import tpu as pltpu
from jax.sharding import PartitionSpec as P

MESH = pl.DeviceIdType.MESH
F32 = jnp.float32
BF16 = jnp.bfloat16
NN = (((1,), (0,)), ((), ()))
NT = (((1,), (1,)), ((), ()))
TN = (((0,), (0,)), ((), ()))


def fourier_basis(count):
    half = count // 2
    place = np.arange(count)
    rows = np.zeros((count, count))
    rows[0] = 1.0 / np.sqrt(count)
    for f in range(1, half):
        rows[f] = np.sqrt(2.0 / count) * np.cos(2.0 * np.pi * (f * place % count) / count)
        rows[half + f] = np.sqrt(2.0 / count) * np.sin(2.0 * np.pi * (f * place % count) / count)
    rows[half] = np.where(place % 2 == 0, 1.0, -1.0) / np.sqrt(count)
    return rows


def split(table):
    high = table.astype(np.float32).astype(ml_dtypes.bfloat16)
    low = (table - high.astype(np.float64)).astype(np.float32).astype(ml_dtypes.bfloat16)
    return np.stack((high, low))


def make_tables(grid, nrow, ncol):
    span_m, span_n = grid // nrow, grid // ncol
    per = 128 // span_n
    groups = span_m // per
    basis = fourier_basis(grid)
    pair = np.zeros((ncol, 128, per * grid))
    for i in range(ncol):
        for u in range(per):
            pair[i, u * span_n:(u + 1) * span_n, u * grid:(u + 1) * grid] = basis[:, i * span_n:(i + 1) * span_n].T
    order = np.arange(grid).reshape(nrow, groups, per).transpose(0, 2, 1).reshape(-1)
    first = basis[:, order]
    return split(basis), split(pair), split(first), split(first.T)


def halves(x):
    high = x.astype(BF16)
    return high, (x - high.astype(F32)).astype(BF16)


def dot_right(x, high, low, dims):
    xh, xl = halves(x)
    dot = functools.partial(lax.dot_general, dimension_numbers=dims, preferred_element_type=F32)
    return dot(xh, high) + (dot(xl, high) + dot(xh, low))


def dot_left(high, low, x, dims):
    xh, xl = halves(x)
    dot = functools.partial(lax.dot_general, dimension_numbers=dims, preferred_element_type=F32)
    return dot(high, xh) + (dot(high, xl) + dot(low, xh))


def encode(x, value_ref, scale_ref):
    top = jnp.max(jnp.abs(x), axis=1, keepdims=True)
    unit = jnp.maximum(top, 1e-30) * (1.0 / 32760.0)
    value_ref[...] = jnp.round(x / unit).astype(jnp.int32).astype(jnp.int16)
    scale_ref[...] = unit[:, 0, :]


def decode(value, scale):
    return value.astype(jnp.int32).astype(F32) * scale[:, None, :]


def field_kernel(nrow, ncol, grid, wide,
                 charge_ref, basis_ref, pair_ref, first_ref, firstt_ref, out_ref,
                 turn, back, *bufs):
    nb = 1 if wide else 2
    stages = [bufs[k * 2 * nb:(k + 1) * 2 * nb] for k in range(4)]
    sems = bufs[8 * nb:]
    my_row, my_col = lax.axis_index("row"), lax.axis_index("col")
    span_m, span_n = grid // nrow, grid // ncol
    per = 128 // span_n
    groups = span_m // per
    thin = span_n // nrow
    barrier = pltpu.get_barrier_semaphore()

    @pl.loop(1, ncol)
    def _(t):
        pl.semaphore_signal(barrier, inc=1, device_id={"col": (my_col + t) % ncol}, device_id_type=MESH)

    @pl.loop(1, nrow)
    def _(t):
        pl.semaphore_signal(barrier, inc=1, device_id={"row": (my_row + t) % nrow}, device_id_type=MESH)

    pl.semaphore_wait(barrier, ncol - 1 + nrow - 1)

    def copies(stage, axis, me, dest, src):
        res = []
        for b in range(nb):
            send, recv = stages[stage][b], stages[stage][nb + b]
            ssem, rsem = sems[stage * 2], sems[stage * 2 + 1]
            res.append(pltpu.make_async_remote_copy(
                src_ref=send.at[dest], dst_ref=recv.at[me],
                send_sem=ssem.at[b, dest], recv_sem=rsem.at[b, src],
                device_id={axis: dest}, device_id_type=MESH))
        return res

    def put(stage, where, rows, x):
        if wide:
            stages[stage][0][where, rows] = x
        else:
            encode(x, stages[stage][0].at[where, rows], stages[stage][1].at[where, rows])

    def get(stage, src, rows):
        if wide:
            return stages[stage][1][src, rows]
        return decode(stages[stage][2][src, rows], stages[stage][3][src, rows])

    def finish(stage, axis, me, count):
        for b in range(nb):
            stages[stage][nb + b][me] = stages[stage][b][me]

        @pl.loop(1, count)
        def _(t):
            src = (me + count - t) % count
            for c in copies(stage, axis, me, src, src):
                c.wait_recv()

        @pl.loop(1, count)
        def _(t):
            dest = (me + t) % count
            for c in copies(stage, axis, me, dest, dest):
                c.wait_send()

    @pl.loop(0, groups)
    def _(k):
        block = charge_ref[pl.ds(pl.multiple_of(k * 128, 128), 128), :]
        turn[k] = dot_left(basis_ref[0], basis_ref[1], block, NT)

    @pl.loop(0, ncol)
    def _(t):
        dest = (my_col + 1 + t) % ncol

        @pl.loop(0, span_n // 16)
        def _(q):
            x = turn[:, pl.ds(pl.multiple_of(dest * span_n + q * 16, 16), 16), :]
            put(0, dest, pl.ds(pl.multiple_of(q * 16, 16), 16), jnp.swapaxes(x, 0, 1))

        @pl.when(t < ncol - 1)
        def _():
            for c in copies(0, "col", my_col, dest, my_col):
                c.start()

    finish(0, "col", my_col, ncol)

    @pl.loop(0, nrow)
    def _(t):
        dest = (my_row + 1 + t) % nrow
        rows = pl.ds(dest * thin, thin)
        acc = jnp.zeros((thin * groups, per * grid), F32)
        for i in range(ncol):
            x = get(0, i, rows).reshape(thin * groups, 128)
            acc = acc + dot_right(x, pair_ref[0, i], pair_ref[1, i], NN)
        parts = [acc[:, u * grid:(u + 1) * grid].reshape(thin, groups, grid) for u in range(per)]
        put(1, dest, slice(None), jnp.concatenate(parts, axis=1))

        @pl.when(t < nrow - 1)
        def _():
            for c in copies(1, "row", my_row, dest, my_row):
                c.start()

    finish(1, "row", my_row, nrow)

    unit = 2.0 * np.pi / grid
    kappa = 8.0 / grid
    half = grid // 2

    def squared(index):
        f = jnp.where(index > half, index - half, index).astype(F32) * unit
        return f * f

    ia = lax.broadcasted_iota(jnp.int32, (grid, grid), 0)
    ib = lax.broadcasted_iota(jnp.int32, (grid, grid), 1)

    @pl.loop(0, thin)
    def _(k):
        x = jnp.concatenate([get(1, s, pl.ds(k, 1))[0] for s in range(nrow)], axis=0)
        y = dot_left(first_ref[0], first_ref[1], x, NN)
        third = my_col * span_n + my_row * thin + k
        ksq = squared(ia) + squared(ib) + squared(third)
        gain = jnp.where((ia + ib + third) == 0, 0.0, (kappa * kappa) / (ksq + kappa * kappa))
        z = dot_left(firstt_ref[0], firstt_ref[1], y * gain, NN)
        for s in range(nrow):
            put(2, s, pl.ds(k, 1), z[None, s * span_m:(s + 1) * span_m])

    @pl.loop(1, nrow)
    def _(t):
        for c in copies(2, "row", my_row, (my_row + t) % nrow, my_row):
            c.start()

    finish(2, "row", my_row, nrow)

    @pl.loop(0, ncol)
    def _(t):
        dest = (my_col + 1 + t) % ncol

        @pl.loop(0, nrow)
        def _(s):
            x = get(2, s, slice(None))
            acc = jnp.zeros((thin * groups, 128), F32)
            for u in range(per):
                xu = x[:, u * groups:(u + 1) * groups].reshape(thin * groups, grid)
                cut = slice(u * grid, (u + 1) * grid)
                acc = acc + dot_right(xu, pair_ref[0, dest, :, cut], pair_ref[1, dest, :, cut], NT)
            put(3, dest, pl.ds(s * thin, thin), acc.reshape(thin, groups, 128))

        @pl.when(t < ncol - 1)
        def _():
            for c in copies(3, "col", my_col, dest, my_col):
                c.start()

    finish(3, "col", my_col, ncol)

    @pl.loop(0, ncol)
    def _(i):
        @pl.loop(0, span_n // 16)
        def _(q):
            rows = pl.ds(pl.multiple_of(q * 16, 16), 16)
            x = get(3, i, rows)
            back[:, pl.ds(pl.multiple_of(i * span_n + q * 16, 16), 16), :] = jnp.swapaxes(x, 0, 1)

    @pl.loop(0, groups)
    def _(k):
        x = dot_right(back[k], basis_ref[0], basis_ref[1], TN)
        out_ref[pl.ds(pl.multiple_of(k * 128, 128), 128), :] = x * (1.0 / (kappa * kappa))


def solve(charge, nrow, ncol, grid, wide):
    span_m, span_n = grid // nrow, grid // ncol
    per = 128 // span_n
    groups = span_m // per
    thin = span_n // nrow
    tables = [jnp.asarray(t) for t in make_tables(grid, nrow, ncol)]
    scratch = [pltpu.VMEM((groups, grid, 128), F32), pltpu.VMEM((groups, grid, 128), F32)]
    col_shape, row_shape = (ncol, span_n, groups, 128), (nrow, thin, span_m, grid)
    for shape in (col_shape, row_shape, row_shape, col_shape):
        for _ in range(2):
            if wide:
                scratch.append(pltpu.VMEM(shape, F32))
            else:
                scratch.append(pltpu.VMEM(shape, jnp.int16))
                scratch.append(pltpu.VMEM(shape[:2] + shape[3:], F32))
    for count in (ncol, nrow, nrow, ncol):
        for _ in range(2):
            scratch.append(pltpu.SemaphoreType.DMA((1 if wide else 2, count)))
    return pl.pallas_call(
        functools.partial(field_kernel, nrow, ncol, grid, wide),
        out_shape=jax.ShapeDtypeStruct((span_m * span_n, grid), F32),
        in_specs=[pl.BlockSpec(memory_space=pltpu.VMEM)] * 5,
        out_specs=pl.BlockSpec(memory_space=pltpu.VMEM),
        scratch_shapes=scratch,
        compiler_params=pltpu.CompilerParams(
            collective_id=0, has_side_effects=True, vmem_limit_bytes=56 * 1024 * 1024),
    )(charge, *tables)


def shards(density_matrix, block_mask, cell_group, electron_shape, ion_charge):
    rows, cols = density_matrix.shape
    brows, bcols = block_mask.shape
    blk = rows // brows
    keep = block_mask.astype(BF16)[:, None, :, None]
    masked = (density_matrix.reshape(brows, blk, bcols, blk) * keep).reshape(rows, cols)
    row_panel = lax.all_gather(masked, "col", axis=1, tiled=True)
    square = jnp.dot(
        row_panel,
        lax.all_gather(masked, "row", axis=0, tiled=True),
        preferred_element_type=F32,
    )
    keep_wide = block_mask.astype(F32)[:, None, :, None]
    update = (2.0 * masked.astype(F32) - square).reshape(brows, blk, bcols, blk) * keep_wide
    next_density = update.reshape(rows, cols).astype(BF16)
    nrow, ncol = lax.axis_size("row"), lax.axis_size("col")
    nblocks = brows * nrow
    row_global = lax.axis_index("row") * rows + jnp.arange(rows, dtype=jnp.int32)
    col_global = lax.axis_index("col") * cols + jnp.arange(cols, dtype=jnp.int32)
    on_diag = row_global[:, None] == col_global[None, :]
    diag_rows = jnp.sum(jnp.where(on_diag, square, 0.0), axis=1)
    local_pop = jnp.sum(diag_rows.reshape(brows, blk), axis=1)
    block_ids = lax.axis_index("row") * brows + jnp.arange(brows, dtype=jnp.int32)
    all_ids = jnp.arange(nblocks, dtype=jnp.int32)
    placed = jnp.sum(
        jnp.where(block_ids[:, None] == all_ids[None, :], local_pop[:, None], 0.0), axis=0
    )
    grid = electron_shape.shape[2]
    population, shape_sum = lax.psum((placed, jnp.sum(electron_shape)), ("row", "col"))
    weight = population * nblocks / jnp.sum(population)
    mean_shape = shape_sum / (grid * grid * grid)
    cell_weight = jnp.sum(
        jnp.where(cell_group[:, :, None] == all_ids[None, None, :], weight[None, None, :], 0.0),
        axis=2,
    )
    charge = cell_weight[:, :, None] * electron_shape / mean_shape - ion_charge
    potential = solve(charge.reshape(-1, grid), nrow, ncol, grid, WIDE)
    return next_density, potential.reshape(electron_shape.shape)


WIDE = False


def solution(mesh):
    in_specs = (
        P("row", "col"),
        P("row", "col"),
        P("row", "col"),
        P("row", "col", None),
        P("row", "col", None),
    )
    out_specs = (P("row", "col"), P("row", "col", None))
    return jax.shard_map(shards, mesh=mesh, in_specs=in_specs, out_specs=out_specs, check_vma=False)
```

```python
import functools

import jax
import jax.numpy as jnp
import ml_dtypes
import numpy as np
from jax import lax
from jax.experimental import pallas as pl
from jax.experimental.pallas import tpu as pltpu
from jax.sharding import PartitionSpec as P

MESH = pl.DeviceIdType.MESH
F32 = jnp.float32
BF16 = jnp.bfloat16
NN = (((1,), (0,)), ((), ()))
NT = (((1,), (1,)), ((), ()))
TN = (((0,), (0,)), ((), ()))


def fourier_basis(count):
    half = count // 2
    place = np.arange(count)
    rows = np.zeros((count, count))
    rows[0] = 1.0 / np.sqrt(count)
    for f in range(1, half):
        rows[f] = np.sqrt(2.0 / count) * np.cos(2.0 * np.pi * (f * place % count) / count)
        rows[half + f] = np.sqrt(2.0 / count) * np.sin(2.0 * np.pi * (f * place % count) / count)
    rows[half] = np.where(place % 2 == 0, 1.0, -1.0) / np.sqrt(count)
    return rows


def split(table):
    high = table.astype(np.float32).astype(ml_dtypes.bfloat16)
    low = (table - high.astype(np.float64)).astype(np.float32).astype(ml_dtypes.bfloat16)
    return np.stack((high, low))


def make_tables(grid, nrow, ncol):
    span_m, span_n = grid // nrow, grid // ncol
    per = 128 // span_n
    groups = span_m // per
    basis = fourier_basis(grid)
    pair = np.zeros((ncol, 128, per * grid))
    for i in range(ncol):
        for u in range(per):
            pair[i, u * span_n:(u + 1) * span_n, u * grid:(u + 1) * grid] = basis[:, i * span_n:(i + 1) * span_n].T
    order = np.arange(grid).reshape(nrow, groups, per).transpose(0, 2, 1).reshape(-1)
    first = basis[:, order]
    return split(basis), split(pair), split(first), split(first.T)


def halves(x):
    high = x.astype(BF16)
    return high, (x - high.astype(F32)).astype(BF16)


def dot_right(x, high, low, dims):
    xh, xl = halves(x)
    dot = functools.partial(lax.dot_general, dimension_numbers=dims, preferred_element_type=F32)
    return dot(xh, high) + (dot(xl, high) + dot(xh, low))


def dot_left(high, low, x, dims):
    xh, xl = halves(x)
    dot = functools.partial(lax.dot_general, dimension_numbers=dims, preferred_element_type=F32)
    return dot(high, xh) + (dot(high, xl) + dot(low, xh))


def encode(x, value_ref, scale_ref):
    top = jnp.max(jnp.abs(x), axis=1, keepdims=True)
    unit = jnp.maximum(top, 1e-30) * (1.0 / 32760.0)
    value_ref[...] = jnp.round(x / unit).astype(jnp.int32).astype(jnp.int16)
    scale_ref[...] = unit[:, 0, :]


def decode(value, scale):
    return value.astype(jnp.int32).astype(F32) * scale[:, None, :]


def field_kernel(nrow, ncol, grid, wide,
                 charge_ref, basis_ref, pair_ref, first_ref, firstt_ref, out_ref,
                 turn, back, *bufs):
    nb = 1 if wide else 2
    stages = [bufs[k * 2 * nb:(k + 1) * 2 * nb] for k in range(4)]
    sems = bufs[8 * nb:]
    my_row, my_col = lax.axis_index("row"), lax.axis_index("col")
    span_m, span_n = grid // nrow, grid // ncol
    per = 128 // span_n
    groups = span_m // per
    thin = span_n // nrow
    barrier = pltpu.get_barrier_semaphore()

    @pl.loop(1, ncol)
    def _(t):
        pl.semaphore_signal(barrier, inc=1, device_id={"col": (my_col + t) % ncol}, device_id_type=MESH)

    @pl.loop(1, nrow)
    def _(t):
        pl.semaphore_signal(barrier, inc=1, device_id={"row": (my_row + t) % nrow}, device_id_type=MESH)

    pl.semaphore_wait(barrier, ncol - 1 + nrow - 1)

    def copies(stage, axis, me, dest, src):
        res = []
        for b in range(nb):
            send, recv = stages[stage][b], stages[stage][nb + b]
            ssem, rsem = sems[stage * 2], sems[stage * 2 + 1]
            res.append(pltpu.make_async_remote_copy(
                src_ref=send.at[dest], dst_ref=recv.at[me],
                send_sem=ssem.at[b, dest], recv_sem=rsem.at[b, src],
                device_id={axis: dest}, device_id_type=MESH))
        return res

    def put(stage, where, rows, x):
        if wide:
            stages[stage][0][where, rows] = x
        else:
            encode(x, stages[stage][0].at[where, rows], stages[stage][1].at[where, rows])

    def get(stage, src, rows):
        if wide:
            return stages[stage][1][src, rows]
        return decode(stages[stage][2][src, rows], stages[stage][3][src, rows])

    def finish(stage, axis, me, count):
        for b in range(nb):
            stages[stage][nb + b][me] = stages[stage][b][me]

        @pl.loop(1, count)
        def _(t):
            src = (me + count - t) % count
            for c in copies(stage, axis, me, src, src):
                c.wait_recv()

        @pl.loop(1, count)
        def _(t):
            dest = (me + t) % count
            for c in copies(stage, axis, me, dest, dest):
                c.wait_send()

    @pl.loop(0, groups)
    def _(k):
        block = charge_ref[pl.ds(pl.multiple_of(k * 128, 128), 128), :]
        turn[k] = dot_left(basis_ref[0], basis_ref[1], block, NT)

    @pl.loop(0, ncol)
    def _(t):
        dest = (my_col + 1 + t) % ncol

        @pl.loop(0, span_n // 16)
        def _(q):
            x = turn[:, pl.ds(pl.multiple_of(dest * span_n + q * 16, 16), 16), :]
            put(0, dest, pl.ds(pl.multiple_of(q * 16, 16), 16), jnp.swapaxes(x, 0, 1))

        @pl.when(t < ncol - 1)
        def _():
            for c in copies(0, "col", my_col, dest, my_col):
                c.start()

    finish(0, "col", my_col, ncol)

    @pl.loop(0, nrow)
    def _(t):
        dest = (my_row + 1 + t) % nrow
        rows = pl.ds(dest * thin, thin)
        acc = jnp.zeros((thin * groups, per * grid), F32)
        for i in range(ncol):
            x = get(0, i, rows).reshape(thin * groups, 128)
            acc = acc + dot_right(x, pair_ref[0, i], pair_ref[1, i], NN)
        parts = [acc[:, u * grid:(u + 1) * grid].reshape(thin, groups, grid) for u in range(per)]
        put(1, dest, slice(None), jnp.concatenate(parts, axis=1))

        @pl.when(t < nrow - 1)
        def _():
            for c in copies(1, "row", my_row, dest, my_row):
                c.start()

    finish(1, "row", my_row, nrow)

    unit = 2.0 * np.pi / grid
    kappa = 8.0 / grid
    half = grid // 2

    def squared(index):
        f = jnp.where(index > half, index - half, index).astype(F32) * unit
        return f * f

    ia = lax.broadcasted_iota(jnp.int32, (grid, grid), 0)
    ib = lax.broadcasted_iota(jnp.int32, (grid, grid), 1)

    @pl.loop(0, thin)
    def _(k):
        x = jnp.concatenate([get(1, s, pl.ds(k, 1))[0] for s in range(nrow)], axis=0)
        y = dot_left(first_ref[0], first_ref[1], x, NN)
        third = my_col * span_n + my_row * thin + k
        ksq = squared(ia) + squared(ib) + squared(third)
        gain = jnp.where((ia + ib + third) == 0, 0.0, (kappa * kappa) / (ksq + kappa * kappa))
        z = dot_left(firstt_ref[0], firstt_ref[1], y * gain, NN)
        for s in range(nrow):
            put(2, s, pl.ds(k, 1), z[None, s * span_m:(s + 1) * span_m])

    @pl.loop(1, nrow)
    def _(t):
        for c in copies(2, "row", my_row, (my_row + t) % nrow, my_row):
            c.start()

    finish(2, "row", my_row, nrow)

    @pl.loop(0, ncol)
    def _(t):
        dest = (my_col + 1 + t) % ncol

        @pl.loop(0, nrow)
        def _(s):
            x = get(2, s, slice(None))
            acc = jnp.zeros((thin * groups, 128), F32)
            for u in range(per):
                xu = x[:, u * groups:(u + 1) * groups].reshape(thin * groups, grid)
                cut = slice(u * grid, (u + 1) * grid)
                acc = acc + dot_right(xu, pair_ref[0, dest, :, cut], pair_ref[1, dest, :, cut], NT)
            put(3, dest, pl.ds(s * thin, thin), acc.reshape(thin, groups, 128))

        @pl.when(t < ncol - 1)
        def _():
            for c in copies(3, "col", my_col, dest, my_col):
                c.start()

    finish(3, "col", my_col, ncol)

    @pl.loop(0, ncol)
    def _(i):
        @pl.loop(0, span_n // 16)
        def _(q):
            rows = pl.ds(pl.multiple_of(q * 16, 16), 16)
            x = get(3, i, rows)
            back[:, pl.ds(pl.multiple_of(i * span_n + q * 16, 16), 16), :] = jnp.swapaxes(x, 0, 1)

    @pl.loop(0, groups)
    def _(k):
        x = dot_right(back[k], basis_ref[0], basis_ref[1], TN)
        out_ref[pl.ds(pl.multiple_of(k * 128, 128), 128), :] = x * (1.0 / (kappa * kappa))


def solve(charge, nrow, ncol, grid, wide):
    span_m, span_n = grid // nrow, grid // ncol
    per = 128 // span_n
    groups = span_m // per
    thin = span_n // nrow
    tables = [jnp.asarray(t) for t in make_tables(grid, nrow, ncol)]
    scratch = [pltpu.VMEM((groups, grid, 128), F32), pltpu.VMEM((groups, grid, 128), F32)]
    col_shape, row_shape = (ncol, span_n, groups, 128), (nrow, thin, span_m, grid)
    for shape in (col_shape, row_shape, row_shape, col_shape):
        for _ in range(2):
            if wide:
                scratch.append(pltpu.VMEM(shape, F32))
            else:
                scratch.append(pltpu.VMEM(shape, jnp.int16))
                scratch.append(pltpu.VMEM(shape[:2] + shape[3:], F32))
    for count in (ncol, nrow, nrow, ncol):
        for _ in range(2):
            scratch.append(pltpu.SemaphoreType.DMA((1 if wide else 2, count)))
    return pl.pallas_call(
        functools.partial(field_kernel, nrow, ncol, grid, wide),
        out_shape=jax.ShapeDtypeStruct((span_m * span_n, grid), F32),
        in_specs=[pl.BlockSpec(memory_space=pltpu.VMEM)] * 5,
        out_specs=pl.BlockSpec(memory_space=pltpu.VMEM),
        scratch_shapes=scratch,
        compiler_params=pltpu.CompilerParams(
            collective_id=0, has_side_effects=True, vmem_limit_bytes=56 * 1024 * 1024),
    )(charge, *tables)


def trace_kernel(nrow, ncol, blk, a_ref, part_ref, out_ref, got, acc, mine, row_in, col_in,
                 tile_send, tile_recv, row_send, row_recv, col_send, col_recv):
    my_row, my_col = lax.axis_index("row"), lax.axis_index("col")
    rows = a_ref.shape[0]
    ratio = nrow // ncol
    inner = rows // blk
    barrier = pltpu.get_barrier_semaphore()

    def place(h):
        other = ratio * my_col + h
        upper = (my_row < other) & ((my_row + other) % 2 == 0)
        lower = (my_row > other) & ((my_row + other) % 2 == 1)
        return other, upper | lower, my_row == other

    @pl.loop(1, ncol)
    def _(t):
        pl.semaphore_signal(barrier, inc=1, device_id={"col": (my_col + t) % ncol}, device_id_type=MESH)

    @pl.loop(1, nrow)
    def _(t):
        pl.semaphore_signal(barrier, inc=1, device_id={"row": (my_row + t) % nrow}, device_id_type=MESH)

    expected = ncol - 1 + nrow - 1
    for h in range(ratio):
        other, sends, same = place(h)
        expected = expected + jnp.where(sends, 1, 0)

        @pl.when(jnp.logical_not(sends | same))
        def _():
            pl.semaphore_signal(barrier, inc=1, device_id={"row": other, "col": my_row // ratio},
                                device_id_type=MESH)

    pl.semaphore_wait(barrier, expected)

    def tile_copy(h, other, slot):
        return pltpu.make_async_remote_copy(
            src_ref=a_ref.at[:, h * rows:(h + 1) * rows], dst_ref=got.at[slot],
            send_sem=tile_send.at[h], recv_sem=tile_recv.at[slot],
            device_id={"row": other, "col": my_row // ratio}, device_id_type=MESH)

    for h in range(ratio):
        other, sends, same = place(h)

        @pl.when(sends)
        def _():
            tile_copy(h, other, my_row % ratio).start()

    acc[...] = part_ref[...]
    lane = lax.broadcasted_iota(jnp.int32, acc.shape, 1)
    line = lax.broadcasted_iota(jnp.int32, acc.shape, 0)
    eye = (lax.broadcasted_iota(jnp.int32, (blk, blk), 0)
           == lax.broadcasted_iota(jnp.int32, (blk, blk), 1))
    for h in range(ratio):
        other, sends, same = place(h)

        @pl.when(same)
        def _():
            got[h] = a_ref[:, h * rows:(h + 1) * rows]

        @pl.when(jnp.logical_not(sends | same))
        def _():
            tile_copy(h, other, h).wait_recv()

        @pl.when(jnp.logical_not(sends))
        def _():
            for g in range(inner):
                for k in range(inner):
                    prod = jnp.dot(
                        a_ref[g * blk:(g + 1) * blk, h * rows + k * blk:h * rows + (k + 1) * blk],
                        got[h, k * blk:(k + 1) * blk, g * blk:(g + 1) * blk],
                        preferred_element_type=F32)
                    value = jnp.sum(jnp.where(eye, prod, 0.0))
                    here = (line == 0) & (lane == my_row * inner + g)
                    there = (line == 0) & (lane == other * inner + k) & (my_row != other)
                    acc[...] += jnp.where(here, value, 0.0) + jnp.where(there, value, 0.0)

    for h in range(ratio):
        other, sends, same = place(h)

        @pl.when(sends)
        def _():
            tile_copy(h, other, my_row % ratio).wait_send()

    def total(axis, me, count, src_ref, slots, send, recv, dst_ref):
        def one(t, who, slot):
            return pltpu.make_async_remote_copy(
                src_ref=src_ref, dst_ref=slots.at[me], send_sem=send.at[t], recv_sem=recv.at[slot],
                device_id={axis: who}, device_id_type=MESH)

        @pl.loop(1, count)
        def _(t):
            one(t, (me + t) % count, me).start()

        slots[me] = src_ref[...]

        @pl.loop(1, count)
        def _(t):
            one(t, (me + t) % count, (me + t) % count).wait_recv()

        dst_ref[...] = jnp.sum(slots[...], axis=0)

        @pl.loop(1, count)
        def _(t):
            one(t, (me + t) % count, me).wait_send()

    total("row", my_row, nrow, acc, row_in, row_send, row_recv, mine)
    total("col", my_col, ncol, mine, col_in, col_send, col_recv, out_ref)


def traces(masked, part, nrow, ncol, blk):
    rows, cols = masked.shape
    ratio = nrow // ncol
    small = (8, 128)
    dma = pltpu.SemaphoreType.DMA
    return pl.pallas_call(
        functools.partial(trace_kernel, nrow, ncol, blk),
        out_shape=jax.ShapeDtypeStruct(small, F32),
        in_specs=[pl.BlockSpec(memory_space=pltpu.VMEM)] * 2,
        out_specs=pl.BlockSpec(memory_space=pltpu.VMEM),
        scratch_shapes=[
            pltpu.VMEM((ratio, rows, rows), BF16), pltpu.VMEM(small, F32), pltpu.VMEM(small, F32),
            pltpu.VMEM((nrow,) + small, F32), pltpu.VMEM((ncol,) + small, F32),
            dma((ratio,)), dma((ratio,)), dma((nrow,)), dma((nrow,)), dma((ncol,)), dma((ncol,)),
        ],
        compiler_params=pltpu.CompilerParams(
            collective_id=1, has_side_effects=True, vmem_limit_bytes=16 * 1024 * 1024),
    )(masked, part)


def shards(density_matrix, block_mask, cell_group, electron_shape, ion_charge):
    rows, cols = density_matrix.shape
    brows, bcols = block_mask.shape
    blk = rows // brows
    grid = electron_shape.shape[2]
    nrow, ncol = lax.axis_size("row"), lax.axis_size("col")
    nblocks = brows * nrow
    keep = block_mask.astype(BF16)[:, None, :, None]
    masked = (density_matrix.reshape(brows, blk, bcols, blk) * keep).reshape(rows, cols)
    row_panel = lax.all_gather(masked, "col", axis=1, tiled=True)
    col_panel = lax.all_gather(masked, "row", axis=0, tiled=True)
    line = jnp.arange(8, dtype=jnp.int32)[:, None]
    lane = jnp.arange(128, dtype=jnp.int32)[None, :]
    part = jnp.where((line == 1) & (lane == 0), jnp.sum(electron_shape), 0.0)
    sums = traces(masked, part, nrow, ncol, blk)
    population, shape_sum = sums[0, :nblocks], sums[1, 0]
    all_ids = jnp.arange(nblocks, dtype=jnp.int32)
    weight = population * nblocks / jnp.sum(population)
    mean_shape = shape_sum / (grid * grid * grid)
    cell_weight = jnp.sum(
        jnp.where(cell_group[:, :, None] == all_ids[None, None, :], weight[None, None, :], 0.0),
        axis=2,
    )
    charge = cell_weight[:, :, None] * electron_shape / mean_shape - ion_charge
    potential = solve(charge.reshape(-1, grid), nrow, ncol, grid, WIDE)
    square = jnp.dot(row_panel, col_panel, preferred_element_type=F32)
    keep_wide = block_mask.astype(F32)[:, None, :, None]
    update = (2.0 * masked.astype(F32) - square).reshape(brows, blk, bcols, blk) * keep_wide
    next_density = update.reshape(rows, cols).astype(BF16)
    return next_density, potential.reshape(electron_shape.shape)


WIDE = False


def solution(mesh):
    in_specs = (
        P("row", "col"),
        P("row", "col"),
        P("row", "col"),
        P("row", "col", None),
        P("row", "col", None),
    )
    out_specs = (P("row", "col"), P("row", "col", None))
    return jax.shard_map(shards, mesh=mesh, in_specs=in_specs, out_specs=out_specs, check_vma=False)
```

```python
import functools

import jax
import jax.numpy as jnp
import ml_dtypes
import numpy as np
from jax import lax
from jax.experimental import pallas as pl
from jax.experimental.pallas import tpu as pltpu
from jax.sharding import PartitionSpec as P

MESH = pl.DeviceIdType.MESH
F32 = jnp.float32
BF16 = jnp.bfloat16
NN = (((1,), (0,)), ((), ()))
NT = (((1,), (1,)), ((), ()))
TN = (((0,), (0,)), ((), ()))


def fourier_basis(count):
    half = count // 2
    place = np.arange(count)
    rows = np.zeros((count, count))
    rows[0] = 1.0 / np.sqrt(count)
    for f in range(1, half):
        rows[f] = np.sqrt(2.0 / count) * np.cos(2.0 * np.pi * (f * place % count) / count)
        rows[half + f] = np.sqrt(2.0 / count) * np.sin(2.0 * np.pi * (f * place % count) / count)
    rows[half] = np.where(place % 2 == 0, 1.0, -1.0) / np.sqrt(count)
    return rows


def split(table):
    high = table.astype(np.float32).astype(ml_dtypes.bfloat16)
    low = (table - high.astype(np.float64)).astype(np.float32).astype(ml_dtypes.bfloat16)
    return np.stack((high, low))


def make_tables(grid, nrow, ncol):
    span_m, span_n = grid // nrow, grid // ncol
    per = 128 // span_n
    groups = span_m // per
    basis = fourier_basis(grid)
    pair = np.zeros((ncol, 128, per * grid))
    for i in range(ncol):
        for u in range(per):
            pair[i, u * span_n:(u + 1) * span_n, u * grid:(u + 1) * grid] = basis[:, i * span_n:(i + 1) * span_n].T
    order = np.arange(grid).reshape(nrow, groups, per).transpose(0, 2, 1).reshape(-1)
    first = basis[:, order]
    return split(basis), split(pair), split(first), split(first.T)


def halves(x):
    high = x.astype(BF16)
    return high, (x - high.astype(F32)).astype(BF16)


def dot_right(x, high, low, dims):
    xh, xl = halves(x)
    dot = functools.partial(lax.dot_general, dimension_numbers=dims, preferred_element_type=F32)
    return dot(xh, high) + (dot(xl, high) + dot(xh, low))


def dot_left(high, low, x, dims):
    xh, xl = halves(x)
    dot = functools.partial(lax.dot_general, dimension_numbers=dims, preferred_element_type=F32)
    return dot(high, xh) + (dot(high, xl) + dot(low, xh))


def encode(x, value_ref, scale_ref):
    top = jnp.max(jnp.abs(x), axis=1, keepdims=True)
    unit = jnp.maximum(top, 1e-30) * (1.0 / 32760.0)
    value_ref[...] = jnp.round(x / unit).astype(jnp.int32).astype(jnp.int16)
    scale_ref[...] = unit[:, 0, :]


def decode(value, scale):
    return value.astype(jnp.int32).astype(F32) * scale[:, None, :]


def field_kernel(nrow, ncol, grid, wide,
                 charge_ref, basis_ref, pair_ref, first_ref, firstt_ref, block_ref,
                 out_ref, panel_ref, turn, back, own_sem, far_send, far_recv, near_send, near_recv, *bufs):
    nb = 1 if wide else 2
    stages = [bufs[k * 2 * nb:(k + 1) * 2 * nb] for k in range(4)]
    sems = bufs[8 * nb:]
    my_row, my_col = lax.axis_index("row"), lax.axis_index("col")
    span_m, span_n = grid // nrow, grid // ncol
    per = 128 // span_n
    groups = span_m // per
    thin = span_n // nrow
    barrier = pltpu.get_barrier_semaphore()

    @pl.loop(1, ncol)
    def _(t):
        pl.semaphore_signal(barrier, inc=1, device_id={"col": (my_col + t) % ncol}, device_id_type=MESH)

    @pl.loop(1, nrow)
    def _(t):
        pl.semaphore_signal(barrier, inc=1, device_id={"row": (my_row + t) % nrow}, device_id_type=MESH)

    pl.semaphore_wait(barrier, ncol - 1 + nrow - 1)

    chips = nrow // 2
    my_chip, core = my_row // 2, my_row % 2
    rows_of = block_ref.shape[0]

    def panel_rows(row):
        return panel_ref.at[pl.ds(pl.multiple_of(row * rows_of, rows_of), rows_of)]

    def far(chip, slot):
        return pltpu.make_async_remote_copy(
            src_ref=block_ref, dst_ref=panel_rows(my_row), send_sem=far_send.at[chip],
            recv_sem=far_recv.at[slot], device_id={"row": 2 * chip + core}, device_id_type=MESH)

    def near(chip, source):
        return pltpu.make_async_remote_copy(
            src_ref=source, dst_ref=panel_rows(2 * chip + core), send_sem=near_send.at[chip],
            recv_sem=near_recv.at[chip], device_id={"row": 2 * my_chip + 1 - core}, device_id_type=MESH)

    own = pltpu.make_async_copy(block_ref, panel_rows(my_row), own_sem)
    own.start()

    @pl.loop(1, chips)
    def _(t):
        far((my_chip + t) % chips, my_chip).start()

    near(my_chip, block_ref).start()

    def copies(stage, axis, me, dest, src):
        res = []
        for b in range(nb):
            send, recv = stages[stage][b], stages[stage][nb + b]
            ssem, rsem = sems[stage * 2], sems[stage * 2 + 1]
            res.append(pltpu.make_async_remote_copy(
                src_ref=send.at[dest], dst_ref=recv.at[me],
                send_sem=ssem.at[b, dest], recv_sem=rsem.at[b, src],
                device_id={axis: dest}, device_id_type=MESH))
        return res

    def put(stage, where, rows, x):
        if wide:
            stages[stage][0][where, rows] = x
        else:
            encode(x, stages[stage][0].at[where, rows], stages[stage][1].at[where, rows])

    def get(stage, src, rows):
        if wide:
            return stages[stage][1][src, rows]
        return decode(stages[stage][2][src, rows], stages[stage][3][src, rows])

    def finish(stage, axis, me, count):
        for b in range(nb):
            stages[stage][nb + b][me] = stages[stage][b][me]

        @pl.loop(1, count)
        def _(t):
            src = (me + count - t) % count
            for c in copies(stage, axis, me, src, src):
                c.wait_recv()

        @pl.loop(1, count)
        def _(t):
            dest = (me + t) % count
            for c in copies(stage, axis, me, dest, dest):
                c.wait_send()

    @pl.loop(0, groups)
    def _(k):
        block = charge_ref[pl.ds(pl.multiple_of(k * 128, 128), 128), :]
        turn[k] = dot_left(basis_ref[0], basis_ref[1], block, NT)

    @pl.loop(0, ncol)
    def _(t):
        dest = (my_col + 1 + t) % ncol

        @pl.loop(0, span_n // 16)
        def _(q):
            x = turn[:, pl.ds(pl.multiple_of(dest * span_n + q * 16, 16), 16), :]
            put(0, dest, pl.ds(pl.multiple_of(q * 16, 16), 16), jnp.swapaxes(x, 0, 1))

        @pl.when(t < ncol - 1)
        def _():
            for c in copies(0, "col", my_col, dest, my_col):
                c.start()

    finish(0, "col", my_col, ncol)

    @pl.loop(0, nrow)
    def _(t):
        dest = (my_row + 1 + t) % nrow
        rows = pl.ds(dest * thin, thin)
        acc = jnp.zeros((thin * groups, per * grid), F32)
        for i in range(ncol):
            x = get(0, i, rows).reshape(thin * groups, 128)
            acc = acc + dot_right(x, pair_ref[0, i], pair_ref[1, i], NN)
        parts = [acc[:, u * grid:(u + 1) * grid].reshape(thin, groups, grid) for u in range(per)]
        put(1, dest, slice(None), jnp.concatenate(parts, axis=1))

        @pl.when(t < nrow - 1)
        def _():
            for c in copies(1, "row", my_row, dest, my_row):
                c.start()

    finish(1, "row", my_row, nrow)

    unit = 2.0 * np.pi / grid
    kappa = 8.0 / grid
    half = grid // 2

    def squared(index):
        f = jnp.where(index > half, index - half, index).astype(F32) * unit
        return f * f

    ia = lax.broadcasted_iota(jnp.int32, (grid, grid), 0)
    ib = lax.broadcasted_iota(jnp.int32, (grid, grid), 1)

    @pl.loop(0, thin)
    def _(k):
        x = jnp.concatenate([get(1, s, pl.ds(k, 1))[0] for s in range(nrow)], axis=0)
        y = dot_left(first_ref[0], first_ref[1], x, NN)
        third = my_col * span_n + my_row * thin + k
        ksq = squared(ia) + squared(ib) + squared(third)
        gain = jnp.where((ia + ib + third) == 0, 0.0, (kappa * kappa) / (ksq + kappa * kappa))
        z = dot_left(firstt_ref[0], firstt_ref[1], y * gain, NN)
        for s in range(nrow):
            put(2, s, pl.ds(k, 1), z[None, s * span_m:(s + 1) * span_m])

    @pl.loop(1, nrow)
    def _(t):
        for c in copies(2, "row", my_row, (my_row + t) % nrow, my_row):
            c.start()

    finish(2, "row", my_row, nrow)

    @pl.loop(1, chips)
    def _(t):
        chip = (my_chip + t) % chips
        far(chip, chip).wait_recv()
        near(chip, panel_rows(2 * chip + core)).start()

    @pl.loop(0, ncol)
    def _(t):
        dest = (my_col + 1 + t) % ncol

        @pl.loop(0, nrow)
        def _(s):
            x = get(2, s, slice(None))
            acc = jnp.zeros((thin * groups, 128), F32)
            for u in range(per):
                xu = x[:, u * groups:(u + 1) * groups].reshape(thin * groups, grid)
                cut = slice(u * grid, (u + 1) * grid)
                acc = acc + dot_right(xu, pair_ref[0, dest, :, cut], pair_ref[1, dest, :, cut], NT)
            put(3, dest, pl.ds(s * thin, thin), acc.reshape(thin, groups, 128))

        @pl.when(t < ncol - 1)
        def _():
            for c in copies(3, "col", my_col, dest, my_col):
                c.start()

    finish(3, "col", my_col, ncol)

    @pl.loop(0, ncol)
    def _(i):
        @pl.loop(0, span_n // 16)
        def _(q):
            rows = pl.ds(pl.multiple_of(q * 16, 16), 16)
            x = get(3, i, rows)
            back[:, pl.ds(pl.multiple_of(i * span_n + q * 16, 16), 16), :] = jnp.swapaxes(x, 0, 1)

    @pl.loop(0, groups)
    def _(k):
        x = dot_right(back[k], basis_ref[0], basis_ref[1], TN)
        out_ref[pl.ds(pl.multiple_of(k * 128, 128), 128), :] = x * (1.0 / (kappa * kappa))

    @pl.loop(1, chips)
    def _(t):
        far((my_chip + t) % chips, my_chip).wait_send()

    @pl.loop(0, chips)
    def _(chip):
        near(chip, block_ref).wait_send()
        near(chip, block_ref).wait_recv()

    own.wait()


def solve(charge, masked, nrow, ncol, grid, wide):
    span_m, span_n = grid // nrow, grid // ncol
    per = 128 // span_n
    groups = span_m // per
    thin = span_n // nrow
    tables = [jnp.asarray(t) for t in make_tables(grid, nrow, ncol)]
    scratch = [pltpu.VMEM((groups, grid, 128), F32), pltpu.VMEM((groups, grid, 128), F32)]
    scratch.append(pltpu.SemaphoreType.DMA(()))
    for _ in range(4):
        scratch.append(pltpu.SemaphoreType.DMA((nrow // 2,)))
    col_shape, row_shape = (ncol, span_n, groups, 128), (nrow, thin, span_m, grid)
    for shape in (col_shape, row_shape, row_shape, col_shape):
        for _ in range(2):
            if wide:
                scratch.append(pltpu.VMEM(shape, F32))
            else:
                scratch.append(pltpu.VMEM(shape, jnp.int16))
                scratch.append(pltpu.VMEM(shape[:2] + shape[3:], F32))
    for count in (ncol, nrow, nrow, ncol):
        for _ in range(2):
            scratch.append(pltpu.SemaphoreType.DMA((1 if wide else 2, count)))
    return pl.pallas_call(
        functools.partial(field_kernel, nrow, ncol, grid, wide),
        out_shape=(jax.ShapeDtypeStruct((span_m * span_n, grid), F32),
                   jax.ShapeDtypeStruct((nrow * masked.shape[0], masked.shape[1]), BF16)),
        in_specs=[pl.BlockSpec(memory_space=pltpu.VMEM)] * 5 + [pl.BlockSpec(memory_space=pl.ANY)],
        out_specs=(pl.BlockSpec(memory_space=pltpu.VMEM), pl.BlockSpec(memory_space=pl.ANY)),
        scratch_shapes=scratch,
        compiler_params=pltpu.CompilerParams(
            collective_id=0, has_side_effects=True, vmem_limit_bytes=56 * 1024 * 1024),
    )(charge, *tables, masked)


def trace_kernel(nrow, ncol, blk, a_ref, part_ref, out_ref, got, acc, mine, row_in, col_in,
                 tile_send, tile_recv, row_send, row_recv, col_send, col_recv):
    my_row, my_col = lax.axis_index("row"), lax.axis_index("col")
    rows = a_ref.shape[0]
    ratio = nrow // ncol
    inner = rows // blk
    barrier = pltpu.get_barrier_semaphore()

    def place(h):
        other = ratio * my_col + h
        upper = (my_row < other) & ((my_row + other) % 2 == 0)
        lower = (my_row > other) & ((my_row + other) % 2 == 1)
        return other, upper | lower, my_row == other

    @pl.loop(1, ncol)
    def _(t):
        pl.semaphore_signal(barrier, inc=1, device_id={"col": (my_col + t) % ncol}, device_id_type=MESH)

    @pl.loop(1, nrow)
    def _(t):
        pl.semaphore_signal(barrier, inc=1, device_id={"row": (my_row + t) % nrow}, device_id_type=MESH)

    expected = ncol - 1 + nrow - 1
    for h in range(ratio):
        other, sends, same = place(h)
        expected = expected + jnp.where(sends, 1, 0)

        @pl.when(jnp.logical_not(sends | same))
        def _():
            pl.semaphore_signal(barrier, inc=1, device_id={"row": other, "col": my_row // ratio},
                                device_id_type=MESH)

    pl.semaphore_wait(barrier, expected)

    def tile_copy(h, other, slot):
        return pltpu.make_async_remote_copy(
            src_ref=a_ref.at[:, h * rows:(h + 1) * rows], dst_ref=got.at[slot],
            send_sem=tile_send.at[h], recv_sem=tile_recv.at[slot],
            device_id={"row": other, "col": my_row // ratio}, device_id_type=MESH)

    for h in range(ratio):
        other, sends, same = place(h)

        @pl.when(sends)
        def _():
            tile_copy(h, other, my_row % ratio).start()

    acc[...] = part_ref[...]
    lane = lax.broadcasted_iota(jnp.int32, acc.shape, 1)
    line = lax.broadcasted_iota(jnp.int32, acc.shape, 0)
    eye = (lax.broadcasted_iota(jnp.int32, (blk, blk), 0)
           == lax.broadcasted_iota(jnp.int32, (blk, blk), 1))
    for h in range(ratio):
        other, sends, same = place(h)

        @pl.when(same)
        def _():
            got[h] = a_ref[:, h * rows:(h + 1) * rows]

        @pl.when(jnp.logical_not(sends | same))
        def _():
            tile_copy(h, other, h).wait_recv()

        @pl.when(jnp.logical_not(sends))
        def _():
            for g in range(inner):
                for k in range(inner):
                    prod = jnp.dot(
                        a_ref[g * blk:(g + 1) * blk, h * rows + k * blk:h * rows + (k + 1) * blk],
                        got[h, k * blk:(k + 1) * blk, g * blk:(g + 1) * blk],
                        preferred_element_type=F32)
                    value = jnp.sum(jnp.where(eye, prod, 0.0))
                    here = (line == 0) & (lane == my_row * inner + g)
                    there = (line == 0) & (lane == other * inner + k) & (my_row != other)
                    acc[...] += jnp.where(here, value, 0.0) + jnp.where(there, value, 0.0)

    for h in range(ratio):
        other, sends, same = place(h)

        @pl.when(sends)
        def _():
            tile_copy(h, other, my_row % ratio).wait_send()

    def total(axis, me, count, src_ref, slots, send, recv, dst_ref):
        def one(t, who, slot):
            return pltpu.make_async_remote_copy(
                src_ref=src_ref, dst_ref=slots.at[me], send_sem=send.at[t], recv_sem=recv.at[slot],
                device_id={axis: who}, device_id_type=MESH)

        @pl.loop(1, count)
        def _(t):
            one(t, (me + t) % count, me).start()

        slots[me] = src_ref[...]

        @pl.loop(1, count)
        def _(t):
            one(t, (me + t) % count, (me + t) % count).wait_recv()

        dst_ref[...] = jnp.sum(slots[...], axis=0)

        @pl.loop(1, count)
        def _(t):
            one(t, (me + t) % count, me).wait_send()

    total("row", my_row, nrow, acc, row_in, row_send, row_recv, mine)
    total("col", my_col, ncol, mine, col_in, col_send, col_recv, out_ref)


def traces(masked, part, nrow, ncol, blk):
    rows, cols = masked.shape
    ratio = nrow // ncol
    small = (8, 128)
    dma = pltpu.SemaphoreType.DMA
    return pl.pallas_call(
        functools.partial(trace_kernel, nrow, ncol, blk),
        out_shape=jax.ShapeDtypeStruct(small, F32),
        in_specs=[pl.BlockSpec(memory_space=pltpu.VMEM)] * 2,
        out_specs=pl.BlockSpec(memory_space=pltpu.VMEM),
        scratch_shapes=[
            pltpu.VMEM((ratio, rows, rows), BF16), pltpu.VMEM(small, F32), pltpu.VMEM(small, F32),
            pltpu.VMEM((nrow,) + small, F32), pltpu.VMEM((ncol,) + small, F32),
            dma((ratio,)), dma((ratio,)), dma((nrow,)), dma((nrow,)), dma((ncol,)), dma((ncol,)),
        ],
        compiler_params=pltpu.CompilerParams(
            collective_id=1, has_side_effects=True, vmem_limit_bytes=16 * 1024 * 1024),
    )(masked, part)


def shards(density_matrix, block_mask, cell_group, electron_shape, ion_charge):
    rows, cols = density_matrix.shape
    brows, bcols = block_mask.shape
    blk = rows // brows
    grid = electron_shape.shape[2]
    nrow, ncol = lax.axis_size("row"), lax.axis_size("col")
    nblocks = brows * nrow
    keep = block_mask.astype(BF16)[:, None, :, None]
    masked = (density_matrix.reshape(brows, blk, bcols, blk) * keep).reshape(rows, cols)
    line = jnp.arange(8, dtype=jnp.int32)[:, None]
    lane = jnp.arange(128, dtype=jnp.int32)[None, :]
    part = jnp.where((line == 1) & (lane == 0), jnp.sum(electron_shape), 0.0)
    sums = traces(masked, part, nrow, ncol, blk)
    later, sums = lax.optimization_barrier((masked, sums))
    row_panel = lax.all_gather(later, "col", axis=1, tiled=True)
    population, shape_sum = sums[0, :nblocks], sums[1, 0]
    all_ids = jnp.arange(nblocks, dtype=jnp.int32)
    weight = population * nblocks / jnp.sum(population)
    mean_shape = shape_sum / (grid * grid * grid)
    cell_weight = jnp.sum(
        jnp.where(cell_group[:, :, None] == all_ids[None, None, :], weight[None, None, :], 0.0),
        axis=2,
    )
    charge = cell_weight[:, :, None] * electron_shape / mean_shape - ion_charge
    potential, col_panel = solve(charge.reshape(-1, grid), masked, nrow, ncol, grid, WIDE)
    square = jnp.dot(row_panel, col_panel, preferred_element_type=F32)
    keep_wide = block_mask.astype(F32)[:, None, :, None]
    update = (2.0 * masked.astype(F32) - square).reshape(brows, blk, bcols, blk) * keep_wide
    next_density = update.reshape(rows, cols).astype(BF16)
    return next_density, potential.reshape(electron_shape.shape)


WIDE = False


def solution(mesh):
    in_specs = (
        P("row", "col"),
        P("row", "col"),
        P("row", "col"),
        P("row", "col", None),
        P("row", "col", None),
    )
    out_specs = (P("row", "col"), P("row", "col", None))
    return jax.shard_map(shards, mesh=mesh, in_specs=in_specs, out_specs=out_specs, check_vma=False)
```

```python
import functools

import jax
import jax.numpy as jnp
import ml_dtypes
import numpy as np
from jax import lax
from jax.experimental import pallas as pl
from jax.experimental.pallas import tpu as pltpu
from jax.sharding import PartitionSpec as P

MESH = pl.DeviceIdType.MESH
F32 = jnp.float32
BF16 = jnp.bfloat16
NN = (((1,), (0,)), ((), ()))
NT = (((1,), (1,)), ((), ()))
TN = (((0,), (0,)), ((), ()))


def fourier_basis(count):
    half = count // 2
    place = np.arange(count)
    rows = np.zeros((count, count))
    rows[0] = 1.0 / np.sqrt(count)
    for f in range(1, half):
        rows[f] = np.sqrt(2.0 / count) * np.cos(2.0 * np.pi * (f * place % count) / count)
        rows[half + f] = np.sqrt(2.0 / count) * np.sin(2.0 * np.pi * (f * place % count) / count)
    rows[half] = np.where(place % 2 == 0, 1.0, -1.0) / np.sqrt(count)
    return rows


def split(table):
    high = table.astype(np.float32).astype(ml_dtypes.bfloat16)
    low = (table - high.astype(np.float64)).astype(np.float32).astype(ml_dtypes.bfloat16)
    return np.stack((high, low))


def make_tables(grid, nrow, ncol):
    span_m, span_n = grid // nrow, grid // ncol
    per = 128 // span_n
    groups = span_m // per
    basis = fourier_basis(grid)
    pair = np.zeros((ncol, 128, per * grid))
    for i in range(ncol):
        for u in range(per):
            pair[i, u * span_n:(u + 1) * span_n, u * grid:(u + 1) * grid] = basis[:, i * span_n:(i + 1) * span_n].T
    order = np.arange(grid).reshape(nrow, groups, per).transpose(0, 2, 1).reshape(-1)
    first = basis[:, order]
    return split(basis), split(pair), split(first), split(first.T)


def halves(x):
    high = x.astype(BF16)
    return high, (x - high.astype(F32)).astype(BF16)


def dot_right(x, high, low, dims):
    xh, xl = halves(x)
    dot = functools.partial(lax.dot_general, dimension_numbers=dims, preferred_element_type=F32)
    return dot(xh, high) + (dot(xl, high) + dot(xh, low))


def dot_left(high, low, x, dims):
    xh, xl = halves(x)
    dot = functools.partial(lax.dot_general, dimension_numbers=dims, preferred_element_type=F32)
    return dot(high, xh) + (dot(high, xl) + dot(low, xh))


def encode(x, value_ref, scale_ref):
    top = jnp.max(jnp.abs(x), axis=1, keepdims=True)
    top = jnp.maximum(top, 1e-30)
    value_ref[...] = jnp.round(x * (32760.0 / top)).astype(jnp.int32).astype(jnp.int16)
    scale_ref[...] = top[:, 0, :] * (1.0 / 32760.0)


def decode(value, scale):
    return value.astype(jnp.int32).astype(F32) * scale[:, None, :]


def field_kernel(nrow, ncol, grid, wide,
                 charge_ref, basis_ref, pair_ref, first_ref, firstt_ref, block_ref,
                 out_ref, panel_ref, turn, back, plain, own_sem, far_send, far_recv, near_send, near_recv, *bufs):
    nb = 1 if wide else 2
    stages = [bufs[k * 2 * nb:(k + 1) * 2 * nb] for k in range(4)]
    sems = bufs[8 * nb:]
    my_row, my_col = lax.axis_index("row"), lax.axis_index("col")
    span_m, span_n = grid // nrow, grid // ncol
    per = 128 // span_n
    groups = span_m // per
    thin = span_n // nrow
    barrier = pltpu.get_barrier_semaphore()

    @pl.loop(1, ncol)
    def _(t):
        pl.semaphore_signal(barrier, inc=1, device_id={"col": (my_col + t) % ncol}, device_id_type=MESH)

    @pl.loop(1, nrow)
    def _(t):
        pl.semaphore_signal(barrier, inc=1, device_id={"row": (my_row + t) % nrow}, device_id_type=MESH)

    pl.semaphore_wait(barrier, ncol - 1 + nrow - 1)

    chips = nrow // 2
    my_chip, core = my_row // 2, my_row % 2
    rows_of = block_ref.shape[0]

    def panel_rows(row):
        return panel_ref.at[pl.ds(pl.multiple_of(row * rows_of, rows_of), rows_of)]

    def far(chip, slot):
        return pltpu.make_async_remote_copy(
            src_ref=block_ref, dst_ref=panel_rows(my_row), send_sem=far_send.at[chip],
            recv_sem=far_recv.at[slot], device_id={"row": 2 * chip + core}, device_id_type=MESH)

    def near(chip, source):
        return pltpu.make_async_remote_copy(
            src_ref=source, dst_ref=panel_rows(2 * chip + core), send_sem=near_send.at[chip],
            recv_sem=near_recv.at[chip], device_id={"row": 2 * my_chip + 1 - core}, device_id_type=MESH)

    own = pltpu.make_async_copy(block_ref, panel_rows(my_row), own_sem)
    own.start()

    @pl.loop(1, chips)
    def _(t):
        far((my_chip + t) % chips, my_chip).start()

    near(my_chip, block_ref).start()

    def copies(stage, axis, me, dest, src):
        res = []
        for b in range(nb):
            send, recv = stages[stage][b], stages[stage][nb + b]
            ssem, rsem = sems[stage * 2], sems[stage * 2 + 1]
            res.append(pltpu.make_async_remote_copy(
                src_ref=send.at[dest], dst_ref=recv.at[me],
                send_sem=ssem.at[b, dest], recv_sem=rsem.at[b, src],
                device_id={axis: dest}, device_id_type=MESH))
        return res

    def put(stage, where, rows, x):
        if wide:
            stages[stage][0][where, rows] = x
        else:
            encode(x, stages[stage][0].at[where, rows], stages[stage][1].at[where, rows])

    def get(stage, src, rows):
        if wide:
            return stages[stage][1][src, rows]
        return decode(stages[stage][2][src, rows], stages[stage][3][src, rows])

    def finish(stage, axis, me, count):
        for b in range(nb):
            stages[stage][nb + b][me] = stages[stage][b][me]

        @pl.loop(1, count)
        def _(t):
            src = (me + count - t) % count
            for c in copies(stage, axis, me, src, src):
                c.wait_recv()

        @pl.loop(1, count)
        def _(t):
            dest = (me + t) % count
            for c in copies(stage, axis, me, dest, dest):
                c.wait_send()

    @pl.loop(0, groups)
    def _(k):
        block = charge_ref[pl.ds(pl.multiple_of(k * 128, 128), 128), :]
        turn[k] = dot_left(basis_ref[0], basis_ref[1], block, NT)

    @pl.loop(0, ncol)
    def _(t):
        dest = (my_col + 1 + t) % ncol

        @pl.loop(0, span_n // 16)
        def _(q):
            x = turn[:, pl.ds(pl.multiple_of(dest * span_n + q * 16, 16), 16), :]
            put(0, dest, pl.ds(pl.multiple_of(q * 16, 16), 16), jnp.swapaxes(x, 0, 1))

        @pl.when(t < ncol - 1)
        def _():
            for c in copies(0, "col", my_col, dest, my_col):
                c.start()

    finish(0, "col", my_col, ncol)

    @pl.loop(0, nrow)
    def _(t):
        dest = (my_row + 1 + t) % nrow
        rows = pl.ds(dest * thin, thin)
        acc = jnp.zeros((thin * groups, per * grid), F32)
        for i in range(ncol):
            x = get(0, i, rows).reshape(thin * groups, 128)
            acc = acc + dot_right(x, pair_ref[0, i], pair_ref[1, i], NN)
        parts = [acc[:, u * grid:(u + 1) * grid].reshape(thin, groups, grid) for u in range(per)]
        put(1, dest, slice(None), jnp.concatenate(parts, axis=1))

        @pl.when(t < nrow - 1)
        def _():
            for c in copies(1, "row", my_row, dest, my_row):
                c.start()

    finish(1, "row", my_row, nrow)

    unit = 2.0 * np.pi / grid
    kappa = 8.0 / grid
    half = grid // 2

    def squared(index):
        f = jnp.where(index > half, index - half, index).astype(F32) * unit
        return f * f

    ia = lax.broadcasted_iota(jnp.int32, (grid, grid), 0)
    ib = lax.broadcasted_iota(jnp.int32, (grid, grid), 1)

    @pl.loop(0, thin)
    def _(k):
        x = jnp.concatenate([get(1, s, pl.ds(k, 1))[0] for s in range(nrow)], axis=0)
        y = dot_left(first_ref[0], first_ref[1], x, NN)
        third = my_col * span_n + my_row * thin + k
        ksq = squared(ia) + squared(ib) + squared(third)
        gain = jnp.where((ia + ib + third) == 0, 0.0, (kappa * kappa) / (ksq + kappa * kappa))
        z = dot_left(firstt_ref[0], firstt_ref[1], y * gain, NN)
        for s in range(nrow):
            put(2, s, pl.ds(k, 1), z[None, s * span_m:(s + 1) * span_m])

    @pl.loop(1, nrow)
    def _(t):
        for c in copies(2, "row", my_row, (my_row + t) % nrow, my_row):
            c.start()

    finish(2, "row", my_row, nrow)

    @pl.loop(1, chips)
    def _(t):
        chip = (my_chip + t) % chips
        far(chip, chip).wait_recv()
        near(chip, panel_rows(2 * chip + core)).start()

    @pl.loop(0, nrow)
    def _(s):
        plain[s] = get(2, s, slice(None))

    @pl.loop(0, ncol)
    def _(t):
        dest = (my_col + 1 + t) % ncol

        @pl.loop(0, nrow)
        def _(s):
            x = plain[s]
            acc = jnp.zeros((thin * groups, 128), F32)
            for u in range(per):
                xu = x[:, u * groups:(u + 1) * groups].reshape(thin * groups, grid)
                cut = slice(u * grid, (u + 1) * grid)
                acc = acc + dot_right(xu, pair_ref[0, dest, :, cut], pair_ref[1, dest, :, cut], NT)
            put(3, dest, pl.ds(s * thin, thin), acc.reshape(thin, groups, 128))

        @pl.when(t < ncol - 1)
        def _():
            for c in copies(3, "col", my_col, dest, my_col):
                c.start()

    finish(3, "col", my_col, ncol)

    @pl.loop(0, ncol)
    def _(i):
        @pl.loop(0, span_n // 16)
        def _(q):
            rows = pl.ds(pl.multiple_of(q * 16, 16), 16)
            x = get(3, i, rows)
            back[:, pl.ds(pl.multiple_of(i * span_n + q * 16, 16), 16), :] = jnp.swapaxes(x, 0, 1)

    @pl.loop(0, groups)
    def _(k):
        x = dot_right(back[k], basis_ref[0], basis_ref[1], TN)
        out_ref[pl.ds(pl.multiple_of(k * 128, 128), 128), :] = x * (1.0 / (kappa * kappa))

    @pl.loop(1, chips)
    def _(t):
        far((my_chip + t) % chips, my_chip).wait_send()

    @pl.loop(0, chips)
    def _(chip):
        near(chip, block_ref).wait_send()
        near(chip, block_ref).wait_recv()

    own.wait()


def solve(charge, masked, nrow, ncol, grid, wide):
    span_m, span_n = grid // nrow, grid // ncol
    per = 128 // span_n
    groups = span_m // per
    thin = span_n // nrow
    tables = [jnp.asarray(t) for t in make_tables(grid, nrow, ncol)]
    scratch = [pltpu.VMEM((groups, grid, 128), F32), pltpu.VMEM((groups, grid, 128), F32)]
    scratch.append(pltpu.VMEM((nrow, thin, span_m, grid), F32))
    scratch.append(pltpu.SemaphoreType.DMA(()))
    for _ in range(4):
        scratch.append(pltpu.SemaphoreType.DMA((nrow // 2,)))
    col_shape, row_shape = (ncol, span_n, groups, 128), (nrow, thin, span_m, grid)
    for shape in (col_shape, row_shape, row_shape, col_shape):
        for _ in range(2):
            if wide:
                scratch.append(pltpu.VMEM(shape, F32))
            else:
                scratch.append(pltpu.VMEM(shape, jnp.int16))
                scratch.append(pltpu.VMEM(shape[:2] + shape[3:], F32))
    for count in (ncol, nrow, nrow, ncol):
        for _ in range(2):
            scratch.append(pltpu.SemaphoreType.DMA((1 if wide else 2, count)))
    return pl.pallas_call(
        functools.partial(field_kernel, nrow, ncol, grid, wide),
        out_shape=(jax.ShapeDtypeStruct((span_m * span_n, grid), F32),
                   jax.ShapeDtypeStruct((nrow * masked.shape[0], masked.shape[1]), BF16)),
        in_specs=[pl.BlockSpec(memory_space=pltpu.VMEM)] * 5 + [pl.BlockSpec(memory_space=pl.ANY)],
        out_specs=(pl.BlockSpec(memory_space=pltpu.VMEM), pl.BlockSpec(memory_space=pl.ANY)),
        scratch_shapes=scratch,
        compiler_params=pltpu.CompilerParams(
            collective_id=0, has_side_effects=True, vmem_limit_bytes=56 * 1024 * 1024),
    )(charge, *tables, masked)


def trace_kernel(nrow, ncol, blk, a_ref, part_ref, out_ref, got, lines, acc, mine, row_in, col_in,
                 tile_send, tile_recv, row_send, row_recv, col_send, col_recv):
    my_row, my_col = lax.axis_index("row"), lax.axis_index("col")
    rows = a_ref.shape[0]
    ratio = nrow // ncol
    inner = rows // blk
    barrier = pltpu.get_barrier_semaphore()

    def place(h):
        other = ratio * my_col + h
        upper = (my_row < other) & ((my_row + other) % 2 == 0)
        lower = (my_row > other) & ((my_row + other) % 2 == 1)
        return other, upper | lower, my_row == other

    @pl.loop(1, ncol)
    def _(t):
        pl.semaphore_signal(barrier, inc=1, device_id={"col": (my_col + t) % ncol}, device_id_type=MESH)

    @pl.loop(1, nrow)
    def _(t):
        pl.semaphore_signal(barrier, inc=1, device_id={"row": (my_row + t) % nrow}, device_id_type=MESH)

    expected = ncol - 1 + nrow - 1
    for h in range(ratio):
        other, sends, same = place(h)
        expected = expected + jnp.where(sends, 1, 0)

        @pl.when(jnp.logical_not(sends | same))
        def _():
            pl.semaphore_signal(barrier, inc=1, device_id={"row": other, "col": my_row // ratio},
                                device_id_type=MESH)

    pl.semaphore_wait(barrier, expected)

    def tile_copy(h, other, slot):
        return pltpu.make_async_remote_copy(
            src_ref=a_ref.at[:, h * rows:(h + 1) * rows], dst_ref=got.at[slot],
            send_sem=tile_send.at[h], recv_sem=tile_recv.at[slot],
            device_id={"row": other, "col": my_row // ratio}, device_id_type=MESH)

    for h in range(ratio):
        other, sends, same = place(h)

        @pl.when(sends)
        def _():
            tile_copy(h, other, my_row % ratio).start()

    acc[...] = part_ref[...]
    eye = (lax.broadcasted_iota(jnp.int32, (blk, blk), 0)
           == lax.broadcasted_iota(jnp.int32, (blk, blk), 1))
    for h in range(ratio):
        other, sends, same = place(h)

        @pl.when(same)
        def _():
            got[h] = a_ref[:, h * rows:(h + 1) * rows]

        @pl.when(jnp.logical_not(sends | same))
        def _():
            tile_copy(h, other, h).wait_recv()

        @pl.when(jnp.logical_not(sends))
        def _():
            for g in range(inner):
                for k in range(inner):
                    prod = jnp.dot(
                        a_ref[g * blk:(g + 1) * blk, h * rows + k * blk:h * rows + (k + 1) * blk],
                        got[h, k * blk:(k + 1) * blk, g * blk:(g + 1) * blk],
                        preferred_element_type=F32)
                    lines[g * inner + k] = jnp.sum(
                        jnp.where(eye, prod, 0.0).reshape(blk // 8, 8, blk), axis=0)
            value = jnp.sum(jnp.sum(lines[...], axis=1, keepdims=True), axis=2, keepdims=True)
            pair = lax.broadcasted_iota(jnp.int32, (inner * inner, 8, 128), 0)
            lane3 = lax.broadcasted_iota(jnp.int32, (inner * inner, 8, 128), 2)
            line3 = lax.broadcasted_iota(jnp.int32, (inner * inner, 8, 128), 1)
            here = (line3 == 0) & (lane3 == my_row * inner + pair // inner)
            there = (line3 == 0) & (lane3 == other * inner + pair % inner) & (my_row != other)
            acc[...] += jnp.sum(jnp.where(here, value, 0.0) + jnp.where(there, value, 0.0), axis=0)

    for h in range(ratio):
        other, sends, same = place(h)

        @pl.when(sends)
        def _():
            tile_copy(h, other, my_row % ratio).wait_send()

    def total(axis, me, count, src_ref, slots, send, recv, dst_ref):
        def one(t, who, slot):
            return pltpu.make_async_remote_copy(
                src_ref=src_ref, dst_ref=slots.at[me], send_sem=send.at[t], recv_sem=recv.at[slot],
                device_id={axis: who}, device_id_type=MESH)

        @pl.loop(1, count)
        def _(t):
            one(t, (me + t) % count, me).start()

        slots[me] = src_ref[...]

        @pl.loop(1, count)
        def _(t):
            one(t, (me + t) % count, (me + t) % count).wait_recv()

        dst_ref[...] = jnp.sum(slots[...], axis=0)

        @pl.loop(1, count)
        def _(t):
            one(t, (me + t) % count, me).wait_send()

    total("row", my_row, nrow, acc, row_in, row_send, row_recv, mine)
    total("col", my_col, ncol, mine, col_in, col_send, col_recv, out_ref)


def traces(masked, part, nrow, ncol, blk):
    rows, cols = masked.shape
    ratio = nrow // ncol
    small = (8, 128)
    dma = pltpu.SemaphoreType.DMA
    return pl.pallas_call(
        functools.partial(trace_kernel, nrow, ncol, blk),
        out_shape=jax.ShapeDtypeStruct(small, F32),
        in_specs=[pl.BlockSpec(memory_space=pltpu.VMEM)] * 2,
        out_specs=pl.BlockSpec(memory_space=pltpu.VMEM),
        scratch_shapes=[
            pltpu.VMEM((ratio, rows, rows), BF16),
            pltpu.VMEM(((rows // blk) ** 2, 8, blk), F32), pltpu.VMEM(small, F32), pltpu.VMEM(small, F32),
            pltpu.VMEM((nrow,) + small, F32), pltpu.VMEM((ncol,) + small, F32),
            dma((ratio,)), dma((ratio,)), dma((nrow,)), dma((nrow,)), dma((ncol,)), dma((ncol,)),
        ],
        compiler_params=pltpu.CompilerParams(
            collective_id=1, has_side_effects=True, vmem_limit_bytes=16 * 1024 * 1024),
    )(masked, part)


def shards(density_matrix, block_mask, cell_group, electron_shape, ion_charge):
    rows, cols = density_matrix.shape
    brows, bcols = block_mask.shape
    blk = rows // brows
    grid = electron_shape.shape[2]
    nrow, ncol = lax.axis_size("row"), lax.axis_size("col")
    nblocks = brows * nrow
    keep = block_mask.astype(BF16)[:, None, :, None]
    masked = (density_matrix.reshape(brows, blk, bcols, blk) * keep).reshape(rows, cols)
    line = jnp.arange(8, dtype=jnp.int32)[:, None]
    lane = jnp.arange(128, dtype=jnp.int32)[None, :]
    part = jnp.where((line == 1) & (lane == 0), jnp.sum(electron_shape), 0.0)
    sums = traces(masked, part, nrow, ncol, blk)
    later, sums = lax.optimization_barrier((masked, sums))
    row_panel = lax.all_gather(later, "col", axis=1, tiled=True)
    population, shape_sum = sums[0, :nblocks], sums[1, 0]
    all_ids = jnp.arange(nblocks, dtype=jnp.int32)
    weight = population * nblocks / jnp.sum(population)
    mean_shape = shape_sum / (grid * grid * grid)
    cell_weight = jnp.sum(
        jnp.where(cell_group[:, :, None] == all_ids[None, None, :], weight[None, None, :], 0.0),
        axis=2,
    )
    charge = cell_weight[:, :, None] * electron_shape / mean_shape - ion_charge
    potential, col_panel = solve(charge.reshape(-1, grid), masked, nrow, ncol, grid, WIDE)
    square = jnp.dot(row_panel, col_panel, preferred_element_type=F32)
    keep_wide = block_mask.astype(F32)[:, None, :, None]
    update = (2.0 * masked.astype(F32) - square).reshape(brows, blk, bcols, blk) * keep_wide
    next_density = update.reshape(rows, cols).astype(BF16)
    return next_density, potential.reshape(electron_shape.shape)


WIDE = False


def solution(mesh):
    in_specs = (
        P("row", "col"),
        P("row", "col"),
        P("row", "col"),
        P("row", "col", None),
        P("row", "col", None),
    )
    out_specs = (P("row", "col"), P("row", "col", None))
    return jax.shard_map(shards, mesh=mesh, in_specs=in_specs, out_specs=out_specs, check_vma=False)
```

```python
import functools

import jax
import jax.numpy as jnp
import ml_dtypes
import numpy as np
from jax import lax
from jax.experimental import pallas as pl
from jax.experimental.pallas import tpu as pltpu
from jax.sharding import PartitionSpec as P

MESH = pl.DeviceIdType.MESH
F32 = jnp.float32
BF16 = jnp.bfloat16
NN = (((1,), (0,)), ((), ()))
NT = (((1,), (1,)), ((), ()))
TN = (((0,), (0,)), ((), ()))


def fourier_basis(count):
    half = count // 2
    place = np.arange(count)
    rows = np.zeros((count, count))
    rows[0] = 1.0 / np.sqrt(count)
    for f in range(1, half):
        rows[f] = np.sqrt(2.0 / count) * np.cos(2.0 * np.pi * (f * place % count) / count)
        rows[half + f] = np.sqrt(2.0 / count) * np.sin(2.0 * np.pi * (f * place % count) / count)
    rows[half] = np.where(place % 2 == 0, 1.0, -1.0) / np.sqrt(count)
    return rows


def split(table):
    high = table.astype(np.float32).astype(ml_dtypes.bfloat16)
    low = (table - high.astype(np.float64)).astype(np.float32).astype(ml_dtypes.bfloat16)
    return np.stack((high, low))


def make_tables(grid, nrow, ncol):
    span_m, span_n = grid // nrow, grid // ncol
    per = 128 // span_n
    groups = span_m // per
    basis = fourier_basis(grid)
    pair = np.zeros((ncol, 128, per * grid))
    for i in range(ncol):
        for u in range(per):
            pair[i, u * span_n:(u + 1) * span_n, u * grid:(u + 1) * grid] = basis[:, i * span_n:(i + 1) * span_n].T
    order = np.arange(grid).reshape(nrow, groups, per).transpose(0, 2, 1).reshape(-1)
    first = basis[:, order]
    return split(basis), split(pair), split(first), split(first.T)


def halves(x):
    high = x.astype(BF16)
    return high, (x - high.astype(F32)).astype(BF16)


def dot_right(x, high, low, dims):
    xh, xl = halves(x)
    dot = functools.partial(lax.dot_general, dimension_numbers=dims, preferred_element_type=F32)
    return dot(xh, high) + (dot(xl, high) + dot(xh, low))


def dot_left(high, low, x, dims):
    xh, xl = halves(x)
    dot = functools.partial(lax.dot_general, dimension_numbers=dims, preferred_element_type=F32)
    return dot(high, xh) + (dot(high, xl) + dot(low, xh))


def encode(x, value_ref, scale_ref):
    top = jnp.max(jnp.abs(x), axis=1, keepdims=True)
    top = jnp.maximum(top, 1e-30)
    value_ref[...] = jnp.round(x * (32760.0 / top)).astype(jnp.int32).astype(jnp.int16)
    scale_ref[...] = top[:, 0, :] * (1.0 / 32760.0)


def decode(value, scale):
    return value.astype(jnp.int32).astype(F32) * scale[:, None, :]


def field_kernel(nrow, ncol, grid, wide,
                 charge_ref, basis_ref, pair_ref, first_ref, firstt_ref, block_ref,
                 out_ref, panel_ref, turn, back, plain, own_sem, far_send, far_recv, near_send, near_recv, *bufs):
    nb = 1 if wide else 2
    stages = [bufs[k * 2 * nb:(k + 1) * 2 * nb] for k in range(4)]
    sems = bufs[8 * nb:]
    my_row, my_col = lax.axis_index("row"), lax.axis_index("col")
    span_m, span_n = grid // nrow, grid // ncol
    per = 128 // span_n
    groups = span_m // per
    thin = span_n // nrow
    barrier = pltpu.get_barrier_semaphore()

    @pl.loop(1, ncol)
    def _(t):
        pl.semaphore_signal(barrier, inc=1, device_id={"col": (my_col + t) % ncol}, device_id_type=MESH)

    @pl.loop(1, nrow)
    def _(t):
        pl.semaphore_signal(barrier, inc=1, device_id={"row": (my_row + t) % nrow}, device_id_type=MESH)

    pl.semaphore_wait(barrier, ncol - 1 + nrow - 1)

    chips = nrow // 2
    my_chip, core = my_row // 2, my_row % 2
    rows_of = block_ref.shape[0]

    def panel_rows(row):
        return panel_ref.at[pl.ds(pl.multiple_of(row * rows_of, rows_of), rows_of)]

    def far(chip, slot):
        return pltpu.make_async_remote_copy(
            src_ref=block_ref, dst_ref=panel_rows(my_row), send_sem=far_send.at[chip],
            recv_sem=far_recv.at[slot], device_id={"row": 2 * chip + core}, device_id_type=MESH)

    def near(chip, source):
        return pltpu.make_async_remote_copy(
            src_ref=source, dst_ref=panel_rows(2 * chip + core), send_sem=near_send.at[chip],
            recv_sem=near_recv.at[chip], device_id={"row": 2 * my_chip + 1 - core}, device_id_type=MESH)

    own = pltpu.make_async_copy(block_ref, panel_rows(my_row), own_sem)
    own.start()

    @pl.loop(1, chips)
    def _(t):
        far((my_chip + t) % chips, my_chip).start()

    near(my_chip, block_ref).start()

    def copies(stage, axis, me, dest, src):
        res = []
        for b in range(nb):
            send, recv = stages[stage][b], stages[stage][nb + b]
            ssem, rsem = sems[stage * 2], sems[stage * 2 + 1]
            res.append(pltpu.make_async_remote_copy(
                src_ref=send.at[dest], dst_ref=recv.at[me],
                send_sem=ssem.at[b, dest], recv_sem=rsem.at[b, src],
                device_id={axis: dest}, device_id_type=MESH))
        return res

    def put(stage, where, rows, x):
        if wide:
            stages[stage][0][where, rows] = x
        else:
            encode(x, stages[stage][0].at[where, rows], stages[stage][1].at[where, rows])

    def get(stage, src, rows):
        if wide:
            return stages[stage][1][src, rows]
        return decode(stages[stage][2][src, rows], stages[stage][3][src, rows])

    def finish(stage, axis, me, count):
        for b in range(nb):
            stages[stage][nb + b][me] = stages[stage][b][me]

        @pl.loop(1, count)
        def _(t):
            src = (me + count - t) % count
            for c in copies(stage, axis, me, src, src):
                c.wait_recv()

        @pl.loop(1, count)
        def _(t):
            dest = (me + t) % count
            for c in copies(stage, axis, me, dest, dest):
                c.wait_send()

    @pl.loop(0, groups)
    def _(k):
        block = charge_ref[pl.ds(pl.multiple_of(k * 128, 128), 128), :]
        turn[k] = dot_left(basis_ref[0], basis_ref[1], block, NT)

    @pl.loop(0, ncol)
    def _(t):
        dest = (my_col + 1 + t) % ncol

        @pl.loop(0, span_n // 16)
        def _(q):
            x = turn[:, pl.ds(pl.multiple_of(dest * span_n + q * 16, 16), 16), :]
            put(0, dest, pl.ds(pl.multiple_of(q * 16, 16), 16), jnp.swapaxes(x, 0, 1))

        @pl.when(t < ncol - 1)
        def _():
            for c in copies(0, "col", my_col, dest, my_col):
                c.start()

    finish(0, "col", my_col, ncol)

    @pl.loop(0, nrow)
    def _(t):
        dest = (my_row + 1 + t) % nrow
        rows = pl.ds(dest * thin, thin)
        acc = jnp.zeros((thin * groups, per * grid), F32)
        for i in range(ncol):
            x = get(0, i, rows).reshape(thin * groups, 128)
            acc = acc + dot_right(x, pair_ref[0, i], pair_ref[1, i], NN)
        parts = [acc[:, u * grid:(u + 1) * grid].reshape(thin, groups, grid) for u in range(per)]
        put(1, dest, slice(None), jnp.concatenate(parts, axis=1))

        @pl.when(t < nrow - 1)
        def _():
            for c in copies(1, "row", my_row, dest, my_row):
                c.start()

    finish(1, "row", my_row, nrow)

    unit = 2.0 * np.pi / grid
    kappa = 8.0 / grid
    half = grid // 2

    def squared(index):
        f = jnp.where(index > half, index - half, index).astype(F32) * unit
        return f * f

    ia = lax.broadcasted_iota(jnp.int32, (grid, grid), 0)
    ib = lax.broadcasted_iota(jnp.int32, (grid, grid), 1)

    @pl.loop(0, thin)
    def _(k):
        x = jnp.concatenate([get(1, s, pl.ds(k, 1))[0] for s in range(nrow)], axis=0)
        y = dot_left(first_ref[0], first_ref[1], x, NN)
        third = my_col * span_n + my_row * thin + k
        ksq = squared(ia) + squared(ib) + squared(third)
        gain = jnp.where((ia + ib + third) == 0, 0.0, (kappa * kappa) / (ksq + kappa * kappa))
        z = dot_left(firstt_ref[0], firstt_ref[1], y * gain, NN)
        for s in range(nrow):
            put(2, s, pl.ds(k, 1), z[None, s * span_m:(s + 1) * span_m])

    @pl.loop(1, nrow)
    def _(t):
        for c in copies(2, "row", my_row, (my_row + t) % nrow, my_row):
            c.start()

    finish(2, "row", my_row, nrow)

    @pl.loop(1, chips)
    def _(t):
        chip = (my_chip + t) % chips
        far(chip, chip).wait_recv()
        near(chip, panel_rows(2 * chip + core)).start()

    @pl.loop(0, nrow)
    def _(s):
        plain[s] = get(2, s, slice(None))

    @pl.loop(0, ncol)
    def _(t):
        dest = (my_col + 1 + t) % ncol

        @pl.loop(0, nrow)
        def _(s):
            x = plain[s]
            acc = jnp.zeros((thin * groups, 128), F32)
            for u in range(per):
                xu = x[:, u * groups:(u + 1) * groups].reshape(thin * groups, grid)
                cut = slice(u * grid, (u + 1) * grid)
                acc = acc + dot_right(xu, pair_ref[0, dest, :, cut], pair_ref[1, dest, :, cut], NT)
            put(3, dest, pl.ds(s * thin, thin), acc.reshape(thin, groups, 128))

        @pl.when(t < ncol - 1)
        def _():
            for c in copies(3, "col", my_col, dest, my_col):
                c.start()

    finish(3, "col", my_col, ncol)

    @pl.loop(0, ncol)
    def _(i):
        @pl.loop(0, span_n // 16)
        def _(q):
            rows = pl.ds(pl.multiple_of(q * 16, 16), 16)
            x = get(3, i, rows)
            back[:, pl.ds(pl.multiple_of(i * span_n + q * 16, 16), 16), :] = jnp.swapaxes(x, 0, 1)

    @pl.loop(0, groups)
    def _(k):
        x = dot_right(back[k], basis_ref[0], basis_ref[1], TN)
        out_ref[pl.ds(pl.multiple_of(k * 128, 128), 128), :] = x * (1.0 / (kappa * kappa))

    @pl.loop(1, chips)
    def _(t):
        far((my_chip + t) % chips, my_chip).wait_send()

    @pl.loop(0, chips)
    def _(chip):
        near(chip, block_ref).wait_send()
        near(chip, block_ref).wait_recv()

    own.wait()


def solve(charge, masked, nrow, ncol, grid, wide):
    span_m, span_n = grid // nrow, grid // ncol
    per = 128 // span_n
    groups = span_m // per
    thin = span_n // nrow
    tables = [jnp.asarray(t) for t in make_tables(grid, nrow, ncol)]
    scratch = [pltpu.VMEM((groups, grid, 128), F32), pltpu.VMEM((groups, grid, 128), F32)]
    scratch.append(pltpu.VMEM((nrow, thin, span_m, grid), F32))
    scratch.append(pltpu.SemaphoreType.DMA(()))
    for _ in range(4):
        scratch.append(pltpu.SemaphoreType.DMA((nrow // 2,)))
    col_shape, row_shape = (ncol, span_n, groups, 128), (nrow, thin, span_m, grid)
    for shape in (col_shape, row_shape, row_shape, col_shape):
        for _ in range(2):
            if wide:
                scratch.append(pltpu.VMEM(shape, F32))
            else:
                scratch.append(pltpu.VMEM(shape, jnp.int16))
                scratch.append(pltpu.VMEM(shape[:2] + shape[3:], F32))
    for count in (ncol, nrow, nrow, ncol):
        for _ in range(2):
            scratch.append(pltpu.SemaphoreType.DMA((1 if wide else 2, count)))
    return pl.pallas_call(
        functools.partial(field_kernel, nrow, ncol, grid, wide),
        out_shape=(jax.ShapeDtypeStruct((span_m * span_n, grid), F32),
                   jax.ShapeDtypeStruct((nrow * masked.shape[0], masked.shape[1]), BF16)),
        in_specs=[pl.BlockSpec(memory_space=pltpu.VMEM)] * 5 + [pl.BlockSpec(memory_space=pl.ANY)],
        out_specs=(pl.BlockSpec(memory_space=pltpu.VMEM), pl.BlockSpec(memory_space=pl.ANY)),
        scratch_shapes=scratch,
        compiler_params=pltpu.CompilerParams(
            collective_id=0, has_side_effects=True, vmem_limit_bytes=56 * 1024 * 1024),
    )(charge, *tables, masked)


def trace_kernel(nrow, ncol, blk, a_ref, part_ref, out_ref, got, lines, acc, mine, row_in, col_in,
                 tile_send, tile_recv, row_send, row_recv, col_send, col_recv):
    my_row, my_col = lax.axis_index("row"), lax.axis_index("col")
    rows = a_ref.shape[0]
    ratio = nrow // ncol
    inner = rows // blk
    barrier = pltpu.get_barrier_semaphore()

    def place(h):
        other = ratio * my_col + h
        upper = (my_row < other) & ((my_row + other) % 2 == 0)
        lower = (my_row > other) & ((my_row + other) % 2 == 1)
        return other, upper | lower, my_row == other

    @pl.loop(1, ncol)
    def _(t):
        pl.semaphore_signal(barrier, inc=1, device_id={"col": (my_col + t) % ncol}, device_id_type=MESH)

    @pl.loop(1, nrow)
    def _(t):
        pl.semaphore_signal(barrier, inc=1, device_id={"row": (my_row + t) % nrow}, device_id_type=MESH)

    expected = ncol - 1 + nrow - 1
    for h in range(ratio):
        other, sends, same = place(h)
        expected = expected + jnp.where(sends, 1, 0)

        @pl.when(jnp.logical_not(sends | same))
        def _():
            pl.semaphore_signal(barrier, inc=1, device_id={"row": other, "col": my_row // ratio},
                                device_id_type=MESH)

    pl.semaphore_wait(barrier, expected)

    def tile_copy(h, other, slot):
        return pltpu.make_async_remote_copy(
            src_ref=a_ref.at[:, h * rows:(h + 1) * rows], dst_ref=got.at[slot],
            send_sem=tile_send.at[h], recv_sem=tile_recv.at[slot],
            device_id={"row": other, "col": my_row // ratio}, device_id_type=MESH)

    for h in range(ratio):
        other, sends, same = place(h)

        @pl.when(sends)
        def _():
            tile_copy(h, other, my_row % ratio).start()

    acc[...] = part_ref[...]
    eye = (lax.broadcasted_iota(jnp.int32, (blk, blk), 0)
           == lax.broadcasted_iota(jnp.int32, (blk, blk), 1))
    for h in range(ratio):
        other, sends, same = place(h)

        @pl.when(same)
        def _():
            got[h] = a_ref[:, h * rows:(h + 1) * rows]

        @pl.when(jnp.logical_not(sends | same))
        def _():
            tile_copy(h, other, h).wait_recv()

        @pl.when(jnp.logical_not(sends))
        def _():
            for g in range(inner):
                for k in range(inner):
                    prod = jnp.dot(
                        a_ref[g * blk:(g + 1) * blk, h * rows + k * blk:h * rows + (k + 1) * blk],
                        got[h, k * blk:(k + 1) * blk, g * blk:(g + 1) * blk],
                        preferred_element_type=F32)
                    lines[g * inner + k] = jnp.sum(
                        jnp.where(eye, prod, 0.0).reshape(blk // 8, 8, blk), axis=0)
            value = jnp.sum(jnp.sum(lines[...], axis=1, keepdims=True), axis=2, keepdims=True)
            pair = lax.broadcasted_iota(jnp.int32, (inner * inner, 8, 128), 0)
            lane3 = lax.broadcasted_iota(jnp.int32, (inner * inner, 8, 128), 2)
            line3 = lax.broadcasted_iota(jnp.int32, (inner * inner, 8, 128), 1)
            here = (line3 == 0) & (lane3 == my_row * inner + pair // inner)
            there = (line3 == 0) & (lane3 == other * inner + pair % inner) & (my_row != other)
            acc[...] += jnp.sum(jnp.where(here, value, 0.0) + jnp.where(there, value, 0.0), axis=0)

    for h in range(ratio):
        other, sends, same = place(h)

        @pl.when(sends)
        def _():
            tile_copy(h, other, my_row % ratio).wait_send()

    def total(axis, me, count, src_ref, slots, send, recv, dst_ref):
        def one(t, who, slot):
            return pltpu.make_async_remote_copy(
                src_ref=src_ref, dst_ref=slots.at[me], send_sem=send.at[t], recv_sem=recv.at[slot],
                device_id={axis: who}, device_id_type=MESH)

        @pl.loop(1, count)
        def _(t):
            one(t, (me + t) % count, me).start()

        slots[me] = src_ref[...]

        @pl.loop(1, count)
        def _(t):
            one(t, (me + t) % count, (me + t) % count).wait_recv()

        dst_ref[...] = jnp.sum(slots[...], axis=0)

        @pl.loop(1, count)
        def _(t):
            one(t, (me + t) % count, me).wait_send()

    total("row", my_row, nrow, acc, row_in, row_send, row_recv, mine)
    total("col", my_col, ncol, mine, col_in, col_send, col_recv, out_ref)


def traces(masked, part, nrow, ncol, blk):
    rows, cols = masked.shape
    ratio = nrow // ncol
    small = (8, 128)
    dma = pltpu.SemaphoreType.DMA
    return pl.pallas_call(
        functools.partial(trace_kernel, nrow, ncol, blk),
        out_shape=jax.ShapeDtypeStruct(small, F32),
        in_specs=[pl.BlockSpec(memory_space=pltpu.VMEM)] * 2,
        out_specs=pl.BlockSpec(memory_space=pltpu.VMEM),
        scratch_shapes=[
            pltpu.VMEM((ratio, rows, rows), BF16),
            pltpu.VMEM(((rows // blk) ** 2, 8, blk), F32), pltpu.VMEM(small, F32), pltpu.VMEM(small, F32),
            pltpu.VMEM((nrow,) + small, F32), pltpu.VMEM((ncol,) + small, F32),
            dma((ratio,)), dma((ratio,)), dma((nrow,)), dma((nrow,)), dma((ncol,)), dma((ncol,)),
        ],
        compiler_params=pltpu.CompilerParams(
            collective_id=1, has_side_effects=True, vmem_limit_bytes=16 * 1024 * 1024),
    )(masked, part)


def shards(density_matrix, block_mask, cell_group, electron_shape, ion_charge):
    rows, cols = density_matrix.shape
    brows, bcols = block_mask.shape
    blk = rows // brows
    grid = electron_shape.shape[2]
    nrow, ncol = lax.axis_size("row"), lax.axis_size("col")
    nblocks = brows * nrow
    keep = block_mask.astype(BF16)[:, None, :, None]
    masked = (density_matrix.reshape(brows, blk, bcols, blk) * keep).reshape(rows, cols)
    line = jnp.arange(8, dtype=jnp.int32)[:, None]
    lane = jnp.arange(128, dtype=jnp.int32)[None, :]
    part = jnp.where((line == 1) & (lane == 0), jnp.sum(electron_shape), 0.0)
    sums = traces(masked, part, nrow, ncol, blk)
    row_panel = lax.all_gather(masked, "col", axis=1, tiled=True)
    population, shape_sum = sums[0, :nblocks], sums[1, 0]
    all_ids = jnp.arange(nblocks, dtype=jnp.int32)
    weight = population * nblocks / jnp.sum(population)
    mean_shape = shape_sum / (grid * grid * grid)
    cell_weight = jnp.sum(
        jnp.where(cell_group[:, :, None] == all_ids[None, None, :], weight[None, None, :], 0.0),
        axis=2,
    )
    charge = cell_weight[:, :, None] * electron_shape / mean_shape - ion_charge
    potential, col_panel = solve(charge.reshape(-1, grid), masked, nrow, ncol, grid, WIDE)
    square = jnp.dot(row_panel, col_panel, preferred_element_type=F32)
    keep_wide = block_mask.astype(F32)[:, None, :, None]
    update = (2.0 * masked.astype(F32) - square).reshape(brows, blk, bcols, blk) * keep_wide
    next_density = update.reshape(rows, cols).astype(BF16)
    return next_density, potential.reshape(electron_shape.shape)


WIDE = False


def solution(mesh):
    in_specs = (
        P("row", "col"),
        P("row", "col"),
        P("row", "col"),
        P("row", "col", None),
        P("row", "col", None),
    )
    out_specs = (P("row", "col"), P("row", "col", None))
    return jax.shard_map(shards, mesh=mesh, in_specs=in_specs, out_specs=out_specs, check_vma=False)
```
